512 devices in a mesh: kpt: 8 (over x, core), orb: 64 (over y, z).
Axes of the slice: x: 4, y: 8, z: 8, core: 2. Of those that a mesh axis runs over, the one named last changes fastest.
Arguments:
- wavefunctions: float32 [8, 64, 102400], P('kpt', 'orb'), may hold values from -8 to 8
- kpoint_vector: float32 [8, 3], P('kpt'), may hold values from -1 to 1
- kpoint_weight: float32 [8], P('kpt'), may hold values from 0.05 to 0.3
- occupation: float32 [48], replicated, may hold values from 0.25 to 2
- orbital_slot: int32 [48], replicated, may hold values from 0 to 63, as said below
- piece_rows: int32 [64], replicated, may hold values from 1 to 20, 640 in all
- external_potential: float32 [8, 6400], P(None, 'orb'), may hold values from -6 to 6
- core_density: float32 [8, 6400], P(None, 'orb'), may hold values from 0.1 to 4
Outputs:
- density: float32 [8, 6400], P(None, 'orb')
- new_orbitals: float32 [8, 48, 204800], P('kpt', None, 'orb')
The draws below stay inside these ranges and needn't reach their ends.
Inputs may be any that keep to these rules, and one draw needn't show every extreme that they name: `orbital_slot`: distinct slot numbers; 0 and 63 are always among them. `piece_rows`: the entries sum to 640.
All inputs are finite; a program needn't handle non-finite values.
Results may differ from the reference program's by a relative error of at most 0.00013.
Values sent between devices are 32-bit elements; how exact they have to be, the bound alone decides.
No kernel may reach another device: no remote copies, remote signals or barrier semaphores. Data moves between devices by JAX's collectives and lax.ppermute only.
A program may use at most 64 MiB of HBM per device.

```python
import math
import jax
import jax.numpy as jnp
import numpy as np
from jax import lax

NX = 80
NY = 80
NZ = 8
ORB = 48
KPT = 8
SLOT_ALL = 64
ROWS = 640
CMAX = 20
N_ORB = 64


def draw_wavefunctions(key, part):
    noise_key, common_key, mixing_key, row_key, slot_key = jax.random.split(key, 5)
    array_shape = (KPT, SLOT_ALL, ROWS, 2 * NX)
    noise_part = jnp.clip(jax.random.normal(noise_key, array_shape, jnp.float32), -4.0, 4.0)
    common = jnp.clip(jax.random.normal(common_key, (KPT, 4, 1, ROWS, 2 * NX), jnp.float32), -4.0, 4.0)
    mixing = jax.random.uniform(mixing_key, (KPT, 4, SLOT_ALL, 1, 1), jnp.float32, -1.0, 1.0)
    shared = mixing[:, 0] * common[:, 0]
    for member in range(1, 4):
        shared = shared + mixing[:, member] * common[:, member]
    row_scale = jnp.exp(jax.random.uniform(row_key, (1, 1, ROWS, 1), jnp.float32, -1.15, 1.15))
    slot_scale = jnp.exp(jax.random.uniform(slot_key, (KPT, SLOT_ALL, 1, 1), jnp.float32, -0.35, 0.35))
    values = (noise_part + 0.5 * shared) * row_scale * slot_scale / jnp.sqrt(jnp.float32(ORB))
    return values.reshape(KPT, SLOT_ALL, ROWS * 2 * NX)


def draw_orbital_slot(key, part):
    first_key, second_key = jax.random.split(key)
    middle = jax.random.permutation(first_key, SLOT_ALL - 2)[:ORB - 2].astype(jnp.int32) + 1
    chosen = jnp.concatenate([jnp.zeros((1,), jnp.int32), middle, jnp.full((1,), SLOT_ALL - 1, jnp.int32)])
    return jax.random.permutation(second_key, chosen).astype(jnp.int32)


def levels(stream_key, shape, cuts, low, top_value):
    factor_of, own = 1.0, jax.random.fold_in(stream_key, 6)
    for position, blocks in cuts:
        heights = jnp.exp(jax.random.uniform(jax.random.fold_in(own, position), (blocks,), jnp.float32, low / len(cuts), top_value / len(cuts)))
        factor_of = factor_of * jnp.repeat(heights, shape[position] // blocks).reshape([-1 if axis == position else 1 for axis in range(len(shape))])
    return factor_of


def split_up(amount, total, reach, slope):
    loads = [(1 << 20) // math.isqrt(grade ** slope) + 1 for grade in range(2, amount + 1)]
    spare, given = total - reach - (amount - 1), [1] * (amount - 1)
    while spare > 0:
        movable = [i for i in range(amount - 1) if given[i] < reach]
        mass, left = sum([loads[i] for i in movable]), spare
        for i in movable:
            addition = min(reach - given[i], max(1, left * loads[i] // mass), spare)
            given[i] = given[i] + addition
            spare = spare - addition
    return np.array([reach] + given)


def uneven(key, count, total, most, skew):
    if count == 2:
        one = jax.random.randint(key, (), max(1, total - most), min(most, total - 1) + 1)
        return jnp.stack([one, total - one])
    tallies = jnp.asarray(split_up(count, total, most, skew), jnp.int32)
    twos = (count - 1) // 2
    giver, sink = tallies[1:1 + 2 * twos:2], tallies[2:2 + 2 * twos:2]
    margin = jnp.minimum(giver - 1, most - sink)
    shifted = jax.random.randint(jax.random.fold_in(key, 1), (twos,), 0, 1 << 20) % (margin + 1)
    tallies = tallies.at[1:1 + 2 * twos:2].set(giver - shifted).at[2:2 + 2 * twos:2].set(sink + shifted)
    return tallies[jax.random.permutation(jax.random.fold_in(key, 2), count)]


def normal_values(own_key, dims, width, reach, cuts=(), kind=jnp.bfloat16):
    values = width * jax.random.normal(own_key, dims, jnp.float32)
    if cuts:
        values = values * levels(own_key, dims, cuts, -0.22, 0.18)
    return jnp.clip(values, -reach, reach).astype(kind)


def setup_inputs(seed: int = 0) -> dict:
    splits = jax.random.split(jax.random.key(seed), 9)
    wavefunctions = draw_wavefunctions(jax.random.fold_in(splits[8], 71), 0)
    kpoint_vector = jnp.clip(jax.random.uniform(splits[1], (KPT, 3), jnp.float32, -1.0, 1.0) * levels(splits[1], (KPT, 3), ((0, 8),), -0.4, 0.0), -1.0, 1.0)
    kpoint_weight = jnp.clip(jnp.exp(math.log(0.3) - 1.7917595 * jax.random.uniform(splits[2], (KPT,), jnp.float32) ** levels(splits[2], (KPT,), ((0, 8),), -0.2, 0.2)), 0.05, 0.3)
    occupation = jnp.clip(jnp.exp(jax.random.uniform(splits[3], (ORB,), jnp.float32, math.log(0.25), math.log(2.0))), 0.25, 2.0)
    orbital_slot = draw_orbital_slot(jax.random.fold_in(splits[8], 71), 0)
    piece_rows = uneven(splits[5], N_ORB, ROWS, CMAX, 2).astype(jnp.int32)
    external_potential = normal_values(splits[6], (NZ, NY * NX), 1.5, 6.0, ((1, 64),), jnp.float32)
    core_density = jnp.clip(jnp.exp(math.log(4.0) - 3.6888794 * jax.random.uniform(splits[7], (NZ, NY * NX), jnp.float32) ** levels(splits[7], (NZ, NY * NX), ((1, 64),), -0.2, 0.2)), 0.1, 4.0)
    return {"wavefunctions": wavefunctions, "kpoint_vector": kpoint_vector, "kpoint_weight": kpoint_weight, "occupation": occupation, "orbital_slot": orbital_slot, "piece_rows": piece_rows, "external_potential": external_potential, "core_density": core_density}


magic_taps = (8.433424733352934e-07, -1.290557201342061e-05, 8.76298447621056e-05, -0.00030158038132690465, 0.001747237136729939, -0.009420470302010804, 0.023738214637249424, 0.0612625895831208, 0.9940415697834004, -0.06048952891969835, -0.021030251609303816, 0.013372634148547948, -0.0034412814449349387, 0.0004944322768868992, -5.185986881173433e-05, 2.7273449291197967e-06)
grid_step = 0.9
half_order = 14
spectrum_center = 13.0
spectrum_half = 17.0
exchange_coef = (3.0 / math.pi) ** (1.0 / 3.0)
exact_mode = lax.Precision.HIGHEST

def stencil_taps():
    factorial = math.factorial
    second_taps = {}
    first_taps = {}
    running = 0.0
    for offset in range(1, half_order + 1):
        weight_j = factorial(half_order) ** 2 / (factorial(half_order - offset) * factorial(half_order + offset))
        tap_sign = (-1.0) ** (offset + 1)
        second_taps[offset] = 2.0 * tap_sign * weight_j / offset ** 2
        second_taps[-offset] = second_taps[offset]
        first_taps[offset] = tap_sign * weight_j / offset
        first_taps[-offset] = -first_taps[offset]
        running = running + 2.0 * second_taps[offset]
    second_taps[0] = -running
    return (second_taps, first_taps)

def band_matrix(length, taps):
    matrix = np.zeros((length, length))
    for offset, tap_value in taps.items():
        matrix = matrix + tap_value * np.eye(length, k=offset)
    return matrix

def axis_tables(length):
    second_taps, first_taps = stencil_taps()
    magic_band = band_matrix(length, {tap_index - 8: magic_taps[tap_index] for tap_index in range(16)})
    return (band_matrix(length, second_taps) * (-0.5 / grid_step ** 2), band_matrix(length, first_taps) / grid_step, magic_band)

def apply_last(grid_field, matrix):
    return jnp.einsum('azyc,dc->azyd', grid_field, matrix, precision=exact_mode)

def apply_rows(grid_field, matrix):
    return jnp.einsum('wy,azyc->azwc', matrix, grid_field, precision=exact_mode)

def apply_planes(grid_field, matrix):
    return jnp.einsum('vz,azyc->avyc', matrix, grid_field, precision=exact_mode)

def swap_halves(values):
    half_width = values.shape[-1] // 2
    return jnp.concatenate([values[..., half_width:], -values[..., :half_width]], axis=-1)

def magic_tables(grid_field):
    half_width = grid_field.shape[3] // 2
    magic_x = jnp.asarray(np.kron(np.eye(2), axis_tables(half_width)[2]), jnp.float32)
    magic_y = jnp.asarray(axis_tables(grid_field.shape[2])[2], jnp.float32)
    magic_z = jnp.asarray(axis_tables(grid_field.shape[1])[2], jnp.float32)
    return (magic_x, magic_y, magic_z)

def magic_forward(grid_field):
    magic_x, magic_y, magic_z = magic_tables(grid_field)
    smooth = apply_last(grid_field, magic_x)
    smooth = apply_rows(smooth, magic_y)
    return apply_planes(smooth, magic_z)

def magic_backward(grid_field):
    magic_x, magic_y, magic_z = magic_tables(grid_field)
    coarse = apply_planes(grid_field, magic_z.T)
    coarse = apply_rows(coarse, magic_y.T)
    return apply_last(coarse, magic_x.T)

def kinetic(grid_field, wave_vector):
    half_width = grid_field.shape[3] // 2
    tables_x = axis_tables(half_width)
    tables_y = axis_tables(grid_field.shape[2])
    tables_z = axis_tables(grid_field.shape[1])
    twist_table = np.array([[0.0, 1.0], [-1.0, 0.0]])
    along_x = jnp.asarray(np.kron(np.eye(2), tables_x[0]), jnp.float32)
    along_x = along_x + wave_vector[0] * jnp.asarray(np.kron(twist_table, tables_x[1]), jnp.float32)
    along_x = along_x + 0.5 * jnp.sum(wave_vector * wave_vector) * jnp.eye(2 * half_width, dtype=jnp.float32)
    stack_y = jnp.stack([jnp.asarray(tables_y[0], jnp.float32), wave_vector[1] * jnp.asarray(tables_y[1], jnp.float32)])
    stack_z = jnp.stack([jnp.asarray(tables_z[0], jnp.float32), wave_vector[2] * jnp.asarray(tables_z[1], jnp.float32)])
    parts_y = jnp.einsum('swy,azyc->sazwc', stack_y, grid_field, precision=exact_mode)
    parts_z = jnp.einsum('svz,azyc->savyc', stack_z, grid_field, precision=exact_mode)
    return apply_last(grid_field, along_x) + parts_y[0] + parts_z[0] + swap_halves(parts_y[1] + parts_z[1])

def potential_pair(potential, planes, rows_y):
    shaped = potential.reshape(planes, rows_y, -1)
    return jnp.concatenate([shaped, shaped], axis=-1)

def chebyshev_image(grid_field, smooth, pair_field, wave_vector):
    applied = kinetic(grid_field, wave_vector) + magic_backward(pair_field[None] * smooth)
    first_term = (applied - spectrum_center * grid_field) / spectrum_half
    applied_again = kinetic(first_term, wave_vector) + magic_backward(pair_field[None] * magic_forward(first_term))
    return applied_again - spectrum_center * first_term

def split_stack(pieces):
    orbital_count, row_count, double_width = pieces.shape
    half_width = double_width // 2
    return pieces.reshape(orbital_count, row_count, 2, half_width).transpose(2, 0, 1, 3).reshape(2 * orbital_count, row_count * half_width)

def gram_of(stacked):
    return jnp.dot(stacked, stacked.T, precision=exact_mode, preferred_element_type=jnp.float32)

def rotate_with(gram_matrix, stacked, components, half_width):
    orbital_count = gram_matrix.shape[0] // 2
    gram_aa = gram_matrix[:orbital_count, :orbital_count]
    gram_ab = gram_matrix[:orbital_count, orbital_count:]
    gram_ba = gram_matrix[orbital_count:, :orbital_count]
    gram_bb = gram_matrix[orbital_count:, orbital_count:]
    over_real = gram_aa + gram_bb
    over_imag = gram_ab - gram_ba
    mean_square = jnp.trace(over_real) / (orbital_count * components) + 1e-06
    shrink_factor = 0.5 / (components * mean_square)
    rot_real = 1.5 * jnp.eye(orbital_count, dtype=jnp.float32) - shrink_factor * over_real
    rot_imag = -shrink_factor * over_imag
    rotation = jnp.concatenate([jnp.concatenate([rot_real, rot_imag], 1), jnp.concatenate([-rot_imag, rot_real], 1)], 0)
    new_stack = jnp.dot(rotation.T, stacked, precision=exact_mode, preferred_element_type=jnp.float32) / jnp.sqrt(mean_square)
    row_count = stacked.shape[1] // half_width
    return new_stack.reshape(2, orbital_count, row_count, half_width).transpose(1, 2, 0, 3).reshape(orbital_count, row_count, 2 * half_width)

def reference(wavefunctions, kpoint_vector, kpoint_weight, occupation, orbital_slot, piece_rows, external_potential, core_density):
    orbitals = jnp.take(wavefunctions, orbital_slot, axis=1).reshape(KPT, ORB, NZ, NY, 2 * NX)

    def density_term(inputs):
        grid_field, weight = inputs
        smooth = magic_forward(grid_field)
        squares = smooth[..., :NX] ** 2 + smooth[..., NX:] ** 2
        return weight * lax.optimization_barrier(jnp.sum(occupation[:, None, None, None] * squares, axis=0))
    density_terms = lax.map(density_term, (orbitals, kpoint_weight))
    density = lax.optimization_barrier(jnp.sum(density_terms, axis=0)).reshape(NZ, NY * NX)
    potential = external_potential - exchange_coef * jnp.power(density + core_density, 1.0 / 3.0)
    pair_field = potential_pair(potential, NZ, NY)
    offsets = (jnp.cumsum(piece_rows) - piece_rows).astype(jnp.int32)
    positions = offsets[:, None] + jnp.arange(CMAX, dtype=jnp.int32)[None, :]
    flat_index = jnp.minimum(positions, ROWS - 1).reshape(-1).astype(jnp.int32)
    flat_valid = (jnp.arange(CMAX, dtype=jnp.int32)[None, :] < piece_rows[:, None]).reshape(-1)

    def wave_step(inputs):
        grid_field, wave_vector = inputs
        smooth = magic_forward(grid_field)
        image_field = chebyshev_image(grid_field, smooth, pair_field, wave_vector)
        filtered = (2.0 * image_field / spectrum_half - grid_field).reshape(ORB, ROWS, 2 * NX)
        stacked = split_stack(filtered)
        rotated = rotate_with(gram_of(stacked), stacked, ROWS * 2 * NX, NX)
        padded = jnp.take(rotated, flat_index, axis=1)
        return jnp.where(flat_valid[None, :, None], padded, 0.0).reshape(ORB, N_ORB * CMAX * 2 * NX)
    new_orbitals = lax.map(wave_step, (orbitals, kpoint_vector))
    return (density, new_orbitals)
```

```python
import math

import jax
import jax.numpy as jnp
import numpy as np
from jax import lax
from jax.sharding import Mesh
from jax.sharding import PartitionSpec as P

NX = 80
NY = 80
NZ = 8

magic_taps = (
    8.433424733352934e-07,
    -1.290557201342061e-05,
    8.76298447621056e-05,
    -0.00030158038132690465,
    0.001747237136729939,
    -0.009420470302010804,
    0.023738214637249424,
    0.0612625895831208,
    0.9940415697834004,
    -0.06048952891969835,
    -0.021030251609303816,
    0.013372634148547948,
    -0.0034412814449349387,
    0.0004944322768868992,
    -5.185986881173433e-05,
    2.7273449291197967e-06,
)
grid_step = 0.9
half_order = 14
spectrum_center = 13.0
spectrum_half = 17.0
exchange_coef = (3.0 / math.pi) ** (1.0 / 3.0)
exact_mode = lax.Precision.HIGHEST


def stencil_taps():
    factorial = math.factorial
    second_taps = {}
    first_taps = {}
    running = 0.0
    for offset in range(1, half_order + 1):
        weight_j = factorial(half_order) ** 2 / (
            factorial(half_order - offset) * factorial(half_order + offset)
        )
        tap_sign = (-1.0) ** (offset + 1)
        second_taps[offset] = 2.0 * tap_sign * weight_j / offset**2
        second_taps[-offset] = second_taps[offset]
        first_taps[offset] = tap_sign * weight_j / offset
        first_taps[-offset] = -first_taps[offset]
        running = running + 2.0 * second_taps[offset]
    second_taps[0] = -running
    return (second_taps, first_taps)


def band_matrix(length, taps):
    matrix = np.zeros((length, length))
    for offset, tap_value in taps.items():
        matrix = matrix + tap_value * np.eye(length, k=offset)
    return matrix


def axis_tables(length):
    second_taps, first_taps = stencil_taps()
    magic_band = band_matrix(
        length, {tap_index - 8: magic_taps[tap_index] for tap_index in range(16)}
    )
    return (
        band_matrix(length, second_taps) * (-0.5 / grid_step**2),
        band_matrix(length, first_taps) / grid_step,
        magic_band,
    )


def apply_last(grid_field, matrix):
    return jnp.einsum("azyc,dc->azyd", grid_field, matrix, precision=exact_mode)


def apply_rows(grid_field, matrix):
    return jnp.einsum("wy,azyc->azwc", matrix, grid_field, precision=exact_mode)


def apply_planes(grid_field, matrix):
    return jnp.einsum("vz,azyc->avyc", matrix, grid_field, precision=exact_mode)


def swap_halves(values):
    half_width = values.shape[-1] // 2
    return jnp.concatenate([values[..., half_width:], -values[..., :half_width]], axis=-1)


def magic_tables(grid_field):
    half_width = grid_field.shape[3] // 2
    magic_x = jnp.asarray(np.kron(np.eye(2), axis_tables(half_width)[2]), jnp.float32)
    magic_y = jnp.asarray(axis_tables(grid_field.shape[2])[2], jnp.float32)
    magic_z = jnp.asarray(axis_tables(grid_field.shape[1])[2], jnp.float32)
    return (magic_x, magic_y, magic_z)


def magic_forward(grid_field):
    magic_x, magic_y, magic_z = magic_tables(grid_field)
    smooth = apply_last(grid_field, magic_x)
    smooth = apply_rows(smooth, magic_y)
    return apply_planes(smooth, magic_z)


def magic_backward(grid_field):
    magic_x, magic_y, magic_z = magic_tables(grid_field)
    coarse = apply_planes(grid_field, magic_z.T)
    coarse = apply_rows(coarse, magic_y.T)
    return apply_last(coarse, magic_x.T)


def kinetic(grid_field, wave_vector):
    half_width = grid_field.shape[3] // 2
    tables_x = axis_tables(half_width)
    tables_y = axis_tables(grid_field.shape[2])
    tables_z = axis_tables(grid_field.shape[1])
    twist_table = np.array([[0.0, 1.0], [-1.0, 0.0]])
    along_x = jnp.asarray(np.kron(np.eye(2), tables_x[0]), jnp.float32)
    along_x = along_x + wave_vector[0] * jnp.asarray(np.kron(twist_table, tables_x[1]), jnp.float32)
    along_x = along_x + 0.5 * jnp.sum(wave_vector * wave_vector) * jnp.eye(
        2 * half_width, dtype=jnp.float32
    )
    stack_y = jnp.stack(
        [
            jnp.asarray(tables_y[0], jnp.float32),
            wave_vector[1] * jnp.asarray(tables_y[1], jnp.float32),
        ]
    )
    stack_z = jnp.stack(
        [
            jnp.asarray(tables_z[0], jnp.float32),
            wave_vector[2] * jnp.asarray(tables_z[1], jnp.float32),
        ]
    )
    parts_y = jnp.einsum("swy,azyc->sazwc", stack_y, grid_field, precision=exact_mode)
    parts_z = jnp.einsum("svz,azyc->savyc", stack_z, grid_field, precision=exact_mode)
    return (
        apply_last(grid_field, along_x)
        + parts_y[0]
        + parts_z[0]
        + swap_halves(parts_y[1] + parts_z[1])
    )


def potential_pair(potential, planes, rows_y):
    shaped = potential.reshape(planes, rows_y, -1)
    return jnp.concatenate([shaped, shaped], axis=-1)


def chebyshev_image(grid_field, smooth, pair_field, wave_vector):
    applied = kinetic(grid_field, wave_vector) + magic_backward(pair_field[None] * smooth)
    first_term = (applied - spectrum_center * grid_field) / spectrum_half
    applied_again = kinetic(first_term, wave_vector) + magic_backward(
        pair_field[None] * magic_forward(first_term)
    )
    return applied_again - spectrum_center * first_term


def split_stack(pieces):
    orbital_count, row_count, double_width = pieces.shape
    half_width = double_width // 2
    return (
        pieces.reshape(orbital_count, row_count, 2, half_width)
        .transpose(2, 0, 1, 3)
        .reshape(2 * orbital_count, row_count * half_width)
    )


def exchange(values, axes):
    return lax.all_to_all(values, axes, split_axis=0, concat_axis=0, tiled=True)


def share(values, count, axes):
    return exchange(jnp.broadcast_to(values[None], (count,) + values.shape), axes)


def on_device(
    wavefunctions,
    kpoint_vector,
    kpoint_weight,
    occupation,
    orbital_slot,
    piece_rows,
    external_potential,
    core_density,
):
    kpt, orb = ("kpt",), ("orb_y", "orb_z")
    kpt_count = lax.axis_size(kpt)
    rank_count = lax.axis_size(orb)
    own_index = lax.axis_index(orb)
    orbital_count = orbital_slot.shape[0]
    capacity = 2 * NZ * NY // rank_count
    slab = NY * NX // rank_count
    grid_field = wavefunctions[0].reshape(1, NZ, NY, 2 * NX)
    wave_vector = kpoint_vector[0]
    ranks = jnp.arange(rank_count, dtype=jnp.int32)
    offsets = jnp.sum(
        jnp.where(ranks[None, :] < ranks[:, None], piece_rows[None, :], 0), axis=1
    )
    positions = jnp.minimum(
        offsets[:, None] + jnp.arange(capacity, dtype=jnp.int32)[None, :], NZ * NY - 1
    ).reshape(-1)
    own_occupation = jnp.sum(jnp.where(orbital_slot == own_index, occupation, 0.0))
    smooth = magic_forward(grid_field)
    squares = smooth[0, ..., :NX] ** 2 + smooth[0, ..., NX:] ** 2
    partial_density = (kpoint_weight[0] * own_occupation * squares).reshape(NZ, rank_count, slab)
    by_owner = partial_density.transpose(1, 0, 2).reshape(rank_count, NZ * slab)
    own_density = jnp.sum(exchange(by_owner, orb), axis=0)
    own_density = jnp.sum(share(own_density, kpt_count, kpt), axis=0)
    slab_density = own_density.reshape(NZ, slab)
    slab_potential = external_potential - exchange_coef * jnp.power(
        slab_density + core_density, 1.0 / 3.0
    )
    potential = share(slab_potential.reshape(NZ * slab), rank_count, orb)
    potential = potential.reshape(rank_count, NZ, slab).transpose(1, 0, 2).reshape(NZ, NY * NX)
    pair_field = potential_pair(potential, NZ, NY)
    image_field = chebyshev_image(grid_field, smooth, pair_field, wave_vector)
    filtered_rows = (2.0 * image_field / spectrum_half - grid_field).reshape(NZ * NY, 2 * NX)
    outgoing = jnp.take(filtered_rows, positions, axis=0).reshape(
        rank_count, capacity * 2 * NX
    )
    received = exchange(outgoing, orb)
    live = (jnp.arange(capacity * 2 * NX, dtype=jnp.int32) // (2 * NX)) < jnp.sum(
        jnp.where(ranks == own_index, piece_rows, 0)
    )
    received = jnp.where(live[None, :], received, 0.0)
    chosen = (orbital_slot[:, None] == ranks[None, :]).astype(jnp.float32)
    pieces = jnp.dot(chosen, received, precision=exact_mode)
    swapped = swap_halves(pieces.reshape(orbital_count, capacity, 2 * NX)).reshape(pieces.shape)
    stacked = jnp.concatenate([pieces, swapped], axis=0)
    gram = lax.dot_general(pieces, stacked, (((1,), (1,)), ((), ())), precision=exact_mode)
    order = jnp.arange(orbital_count)
    upper = order[:, None] <= order[None, :]
    packed = jnp.where(upper, gram[:, :orbital_count], gram[:, orbital_count:])
    packed = packed.reshape(-1)
    for axis in ("orb_z", "orb_y"):
        packed = jnp.sum(share(packed, lax.axis_size(axis), (axis,)), axis=0)
    packed = packed.reshape(orbital_count, orbital_count)
    over_real = jnp.where(upper, packed, packed.T)
    over_imag = jnp.where(upper, -packed.T, packed)
    over_imag = jnp.where(jnp.eye(orbital_count, dtype=bool), 0.0, over_imag)
    components = NZ * NY * 2 * NX
    mean_square = jnp.trace(over_real) / (orbital_count * components) + 1e-06
    shrink_factor = 0.5 / (components * mean_square)
    rot_real = 1.5 * jnp.eye(orbital_count, dtype=jnp.float32) - shrink_factor * over_real
    rot_imag = -shrink_factor * over_imag
    rotation = jnp.concatenate([rot_real.T, -rot_imag.T], axis=1) / jnp.sqrt(mean_square)
    new_rows = jnp.dot(rotation, stacked, precision=exact_mode)
    return (slab_density, new_rows[None])


def solution(mesh):
    side = math.isqrt(mesh.shape["orb"])
    fine = Mesh(
        mesh.devices.reshape(mesh.shape["kpt"], -1, side), ("kpt", "orb_y", "orb_z")
    )
    orb = ("orb_y", "orb_z")
    in_specs = (
        P("kpt", orb, None),
        P("kpt", None),
        P("kpt"),
        P(),
        P(),
        P(),
        P(None, orb),
        P(None, orb),
    )
    out_specs = (P(None, orb), P("kpt", None, orb))
    return jax.shard_map(
        on_device, mesh=fine, in_specs=in_specs, out_specs=out_specs, check_vma=False
    )
```

```python
import math

import jax
import jax.numpy as jnp
import numpy as np
from jax import lax
from jax.experimental import pallas as pl
from jax.experimental.pallas import tpu as pltpu
from jax.sharding import Mesh
from jax.sharding import PartitionSpec as P

NX = 80
NY = 80
NZ = 8
ROWS = NZ * NY
LANES = 128
WIDE = 2 * LANES
SLAB = 100
GROUP = 64

magic_taps = (
    8.433424733352934e-07,
    -1.290557201342061e-05,
    8.76298447621056e-05,
    -0.00030158038132690465,
    0.001747237136729939,
    -0.009420470302010804,
    0.023738214637249424,
    0.0612625895831208,
    0.9940415697834004,
    -0.06048952891969835,
    -0.021030251609303816,
    0.013372634148547948,
    -0.0034412814449349387,
    0.0004944322768868992,
    -5.185986881173433e-05,
    2.7273449291197967e-06,
)
grid_step = 0.9
half_order = 14
spectrum_center = 13.0
spectrum_half = 17.0
exchange_coef = (3.0 / math.pi) ** (1.0 / 3.0)


def stencil_taps():
    factorial = math.factorial
    second_taps = {}
    first_taps = {}
    running = 0.0
    for offset in range(1, half_order + 1):
        weight_j = factorial(half_order) ** 2 / (
            factorial(half_order - offset) * factorial(half_order + offset)
        )
        tap_sign = (-1.0) ** (offset + 1)
        second_taps[offset] = 2.0 * tap_sign * weight_j / offset**2
        second_taps[-offset] = second_taps[offset]
        first_taps[offset] = tap_sign * weight_j / offset
        first_taps[-offset] = -first_taps[offset]
        running = running + 2.0 * second_taps[offset]
    second_taps[0] = -running
    return (second_taps, first_taps)


def band_matrix(length, taps):
    matrix = np.zeros((length, length))
    for offset, tap_value in taps.items():
        matrix = matrix + tap_value * np.eye(length, k=offset)
    return matrix


def axis_tables(length):
    second_taps, first_taps = stencil_taps()
    magic_band = band_matrix(
        length, {tap_index - 8: magic_taps[tap_index] for tap_index in range(16)}
    )
    return (
        band_matrix(length, second_taps) * (-0.5 / grid_step**2),
        band_matrix(length, first_taps) / grid_step,
        magic_band,
    )


def split_table(matrix):
    matrix = np.asarray(matrix, np.float32)
    high = matrix.astype(jnp.bfloat16)
    low = (matrix - high.astype(np.float32)).astype(jnp.bfloat16)
    return high, low


def lane_table(blocks):
    table = np.zeros((WIDE, WIDE))
    for (row, column), block in blocks.items():
        r, c = row * LANES, column * LANES
        table[r : r + NX, c : c + NX] = block
    return table


def tables():
    second_x, first_x, magic_x = axis_tables(NX)
    second_y, first_y, magic_y = axis_tables(NY)

    def packed(matrix):
        high, low = split_table(matrix)
        return np.concatenate([high, low, high], axis=1)

    return {
        "x_second": lane_table({(0, 0): second_x.T, (1, 1): second_x.T}).astype(np.float32),
        "x_first": lane_table({(1, 0): first_x.T, (0, 1): -first_x.T}).astype(np.float32),
        "x_magic": np.stack(split_table(lane_table({(0, 0): magic_x.T, (1, 1): magic_x.T}))),
        "x_magic_back": np.stack(split_table(lane_table({(0, 0): magic_x, (1, 1): magic_x}))),
        "y_all": packed(np.concatenate([magic_y, second_y, first_y], axis=0)),
        "y_back": packed(magic_y.T),
    }


def split(values):
    high = values.astype(jnp.bfloat16)
    low = (values - high.astype(jnp.float32)).astype(jnp.bfloat16)
    return high, low


def mul(left, right):
    return jnp.dot(left, right, preferred_element_type=jnp.float32)


def twist(values):
    return jnp.concatenate([values[:, LANES:], -values[:, :LANES]], axis=1)


def lanes_of(rows):
    return lax.broadcasted_iota(jnp.int32, (rows, LANES), 1)


def roll(values, shift):
    shift = shift % LANES
    return pltpu.roll(values, shift, 1) if shift else values


def compose(lane, parts):
    result = parts[-1][1]
    for end, values in reversed(parts[:-1]):
        result = jnp.where(lane < end, values, result)
    return result


def x_weights(vector_ref, second_ref, first_ref, weight_ref):
    qx, qy, qz = (vector_ref[0, d] for d in range(3))
    shift = 0.5 * (qx * qx + qy * qy + qz * qz)
    row = lax.broadcasted_iota(jnp.int32, (WIDE, WIDE), 0)
    column = lax.broadcasted_iota(jnp.int32, (WIDE, WIDE), 1)
    weights = second_ref[...] + qx * first_ref[...]
    weights = weights + jnp.where(row == column, shift, 0.0)
    high, low = split(weights)
    weight_ref[0] = high
    weight_ref[1] = low


def x_product(values, weight_ref):
    high, low = split(values)
    return mul(high, weight_ref[0]) + mul(high, weight_ref[1]) + mul(low, weight_ref[0])


def y_product(table_ref, values):
    high, low = split(values)
    return mul(table_ref[...], jnp.concatenate([high, high, low], axis=0))


CHUNK = 160


def forward_xy(vector_ref, field_ref, kinetic_ref, smooth_ref, y_all_ref, weight_ref, x_magic_ref):
    qy = vector_ref[0, 1]
    for z in range(NZ):
        rows = slice(z * NY, (z + 1) * NY)
        product = y_product(y_all_ref, field_ref[rows, :])
        smooth_ref[rows, :] = product[:NY]
        kinetic_ref[rows, :] = product[NY : 2 * NY] + twist(qy * product[2 * NY :])
    for start in range(0, ROWS, CHUNK):
        rows = slice(start, start + CHUNK)
        kinetic_ref[rows, :] += x_product(field_ref[rows, :], weight_ref)
        smooth_ref[rows, :] = x_product(smooth_ref[rows, :], x_magic_ref)


def z_sum(matrix, planes):
    results = []
    for v in range(NZ):
        total = None
        for z in range(NZ):
            if matrix[v, z] != 0.0:
                term = float(matrix[v, z]) * planes[z]
                total = term if total is None else total + term
        results.append(total)
    return results


def z_kinetic(vector_ref, field_ref, kinetic_ref, y):
    second_z, first_z, _ = axis_tables(NZ)
    qz = vector_ref[0, 2]
    planes = [field_ref[z * NY + y : z * NY + y + 8, :] for z in range(NZ)]
    turned = [qz * twist(p) for p in planes]
    for z, (a, b) in enumerate(zip(z_sum(second_z, planes), z_sum(first_z, turned))):
        kinetic_ref[z * NY + y : z * NY + y + 8, :] += a + b


def density_kernel(
    rank_ref,
    weight_k_ref,
    occupation_ref,
    slot_ref,
    vector_ref,
    linear_ref,
    second_ref,
    first_ref,
    x_magic_ref,
    y_all_ref,
    field_ref,
    kinetic_ref,
    smooth_ref,
    out_ref,
    parts_ref,
    weight_ref,
    rows_ref,
):
    x_weights(vector_ref, second_ref, first_ref, weight_ref)
    lane = lanes_of(ROWS // 4)
    tiles = [linear_ref[pl.ds(t, ROWS // 4, stride=5), :] for t in range(5)]
    for h in range(8):
        t, start = divmod(NX * h, LANES)
        base = tiles[t]
        if start + NX > LANES:
            base = jnp.where(lane >= start, base, tiles[t + 1])
        piece = jnp.where(lane < NX, roll(base, -start), 0.0)
        parts_ref[h % 2, pl.ds(h // 2, ROWS // 4, stride=4), :] = piece
    field_ref[:, :LANES] = parts_ref[0]
    field_ref[:, LANES:] = parts_ref[1]
    forward_xy(
        vector_ref, field_ref, kinetic_ref, smooth_ref, y_all_ref, weight_ref, x_magic_ref
    )
    scale = jnp.float32(0.0)
    for i in range(slot_ref.shape[0]):
        scale = scale + jnp.where(slot_ref[i] == rank_ref[0], occupation_ref[i], 0.0)
    scale = scale * weight_k_ref[0]
    magic_z = axis_tables(NZ)[2]
    for y in range(0, NY, 8):
        z_kinetic(vector_ref, field_ref, kinetic_ref, y)
        planes = [smooth_ref[z * NY + y : z * NY + y + 8, :] for z in range(NZ)]
        for z, plane in enumerate(z_sum(magic_z, planes)):
            smooth_ref[z * NY + y : z * NY + y + 8, :] = plane
            real, imaginary = plane[:, :LANES], plane[:, LANES:]
            rows_ref[z * NY + y : z * NY + y + 8, :] = scale * (
                real * real + imaginary * imaginary
            )
    groups = ROWS // 5
    lane = lanes_of(groups)
    rows = [rows_ref[pl.ds(t, groups, stride=5), :] for t in range(5)]
    for s in range(4):
        slab = jnp.where(
            lane < NX * (s + 1) - SLAB * s,
            roll(rows[s], NX * s - SLAB * s),
            roll(rows[s + 1], NX * (s + 1) - SLAB * s),
        )
        for z in range(NZ):
            out_ref[pl.ds(8 * s + z, 16, stride=32), :] = slab[16 * z : 16 * z + 16]


def total_kernel(in_ref, out_ref):
    total = in_ref[0]
    for i in range(1, in_ref.shape[0]):
        total = total + in_ref[i]
    for i in range(out_ref.shape[0]):
        out_ref[i] = total


def potential_kernel(in_ref, external_ref, core_ref, density_ref, out_ref, pad_ref):
    total = in_ref[0]
    for i in range(1, in_ref.shape[0]):
        total = total + in_ref[i]
    density = total[:, :SLAB]
    density_ref[...] = density
    root = jnp.exp(jnp.log(density + core_ref[...]) * (1.0 / 3.0))
    pad_ref[...] = jnp.zeros_like(pad_ref)
    pad_ref[:, :SLAB] = external_ref[...] - exchange_coef * root
    padded = pad_ref[...]
    for i in range(out_ref.shape[0]):
        out_ref[i] = padded


def filter_kernel(
    count_ref,
    vector_ref,
    field_ref,
    kinetic_ref,
    smooth_ref,
    slabs_ref,
    second_ref,
    first_ref,
    x_magic_ref,
    x_back_ref,
    y_all_ref,
    y_back_ref,
    out_ref,
    potential_ref,
    weight_ref,
    term_ref,
    wave_ref,
    kin_ref,
    work_ref,
    parts_ref,
    owned_ref,
):
    x_weights(vector_ref, second_ref, first_ref, weight_ref)
    lane = lanes_of(16)
    for z in range(NZ):
        slabs = [slabs_ref[pl.ds(8 * s + z, 16, stride=32), :] for s in range(4)]
        for t in range(5):
            if t == 0:
                row = slabs[0]
            elif t == 4:
                row = roll(slabs[3], SLAB * 3 - NX * 4)
            else:
                row = jnp.where(
                    lane < SLAB * t - NX * t,
                    roll(slabs[t - 1], SLAB * (t - 1) - NX * t),
                    roll(slabs[t], SLAB * t - NX * t),
                )
            potential_ref[pl.ds(z * NY + t, 16, stride=5), :] = row
    magic_z = axis_tables(NZ)[2]

    def weighted(planes, y):
        result = []
        for z, plane in enumerate(planes):
            potential = potential_ref[z * NY + y : z * NY + y + 8, :]
            result.append(plane * jnp.concatenate([potential, potential], axis=1))
        return result

    def backward(values_ref):
        for z in range(NZ):
            rows = slice(z * NY, (z + 1) * NY)
            values_ref[rows, :] = y_product(y_back_ref, values_ref[rows, :])

    for y in range(0, NY, 8):
        planes = [smooth_ref[z * NY + y : z * NY + y + 8, :] for z in range(NZ)]
        for z, plane in enumerate(z_sum(magic_z.T, weighted(planes, y))):
            work_ref[z * NY + y : z * NY + y + 8, :] = plane
    backward(work_ref)
    for start in range(0, ROWS, CHUNK):
        rows = slice(start, start + CHUNK)
        applied = kinetic_ref[rows, :] + x_product(work_ref[rows, :], x_back_ref)
        term_ref[rows, :] = (applied - spectrum_center * field_ref[rows, :]) * (
            1.0 / spectrum_half
        )
    forward_xy(vector_ref, term_ref, kin_ref, wave_ref, y_all_ref, weight_ref, x_magic_ref)
    for y in range(0, NY, 8):
        z_kinetic(vector_ref, term_ref, kin_ref, y)
        planes = [wave_ref[z * NY + y : z * NY + y + 8, :] for z in range(NZ)]
        planes = weighted(z_sum(magic_z, planes), y)
        for z, plane in enumerate(z_sum(magic_z.T, planes)):
            work_ref[z * NY + y : z * NY + y + 8, :] = plane
    backward(work_ref)
    for start in range(0, ROWS, CHUNK):
        rows = slice(start, start + CHUNK)
        image = kin_ref[rows, :] + x_product(work_ref[rows, :], x_back_ref)
        image = image - spectrum_center * term_ref[rows, :]
        filtered = (2.0 / spectrum_half) * image - field_ref[rows, :]
        parts_ref[0, rows, :] = filtered[:, :LANES]
        parts_ref[1, rows, :] = filtered[:, LANES:]
    parts_ref[:, ROWS:, :] = jnp.zeros((2, parts_ref.shape[1] - ROWS, LANES), jnp.float32)
    offset = 0
    for d in range(GROUP):
        for part in range(2):
            owned_ref[part, 24 * d : 24 * d + 24, :] = parts_ref[part, pl.ds(offset, 24), :]
        offset = offset + count_ref[d]
    lane = lanes_of(GROUP)
    for q in range(5):
        pieces = [
            roll(owned_ref[h % 2, pl.ds(4 * q + h // 2, GROUP, stride=24), :], NX * h)
            for h in range(8)
        ]
        for t in range(5):
            first, last = LANES * t // NX, (LANES * t + LANES - 1) // NX
            parts = [(NX * (h + 1) - LANES * t, pieces[h]) for h in range(first, last + 1)]
            out_ref[pl.ds(5 * q + t, GROUP, stride=25), :] = compose(lane, parts)


def gram_kernel(rank_ref, count_ref, slot_ref, in_ref, stack_ref, out_ref, chosen_ref):
    orbitals = slot_ref.shape[0]
    for i in range(orbitals):
        chosen_ref[pl.ds(i, 25, stride=orbitals), :] = in_ref[pl.ds(25 * slot_ref[i], 25), :]
    limit = 2 * NX * count_ref[rank_ref[0]]
    lane = lanes_of(orbitals)
    total = jnp.zeros((2 * orbitals, WIDE), jnp.float32)
    empty = jnp.zeros((64 - orbitals, LANES), jnp.bfloat16)
    for q in range(5):
        tiles = []
        for t in range(5):
            place = 5 * q + t
            tile = chosen_ref[place * orbitals : (place + 1) * orbitals, :]
            tiles.append(jnp.where(lane < limit - LANES * place, tile, 0.0))
        ahead = [roll(tile, -NX) for tile in tiles]
        behind = [roll(tile, NX) for tile in tiles]
        lefts, rights = [], []
        for t in range(5):
            parts, position = [], LANES * t
            while position < LANES * (t + 1):
                h = position // NX
                shift = NX if h % 2 == 0 else -NX
                source = (position + shift) // LANES
                end = min(
                    NX * (h + 1), LANES * (source + 1) - shift, LANES * (t + 1)
                )
                values = ahead[source] if h % 2 == 0 else -behind[source]
                parts.append((end - LANES * t, values))
                position = end
            turned = compose(lane, parts)
            high, low = split(tiles[t])
            turned_high, turned_low = split(turned)
            right = jnp.concatenate(
                [high, empty, turned_high, empty, low, empty, turned_low, empty], axis=0
            )
            stack_ref[5 * q + t] = right
            lefts.append(jnp.concatenate([high, low], axis=0))
            rights.append(right)
        total = total + lax.dot_general(
            jnp.concatenate(lefts, axis=1),
            jnp.concatenate(rights, axis=1),
            (((1,), (1,)), ((), ())),
            preferred_element_type=jnp.float32,
        )
    both = total[:orbitals, :LANES] + (
        total[orbitals:, :LANES] + total[:orbitals, LANES:]
    )
    row = lax.broadcasted_iota(jnp.int32, (orbitals, LANES), 0)
    packed = jnp.where(row <= lane, both, roll(both, 64))
    half = orbitals // 2
    lane = lanes_of(half)
    folded = jnp.where(lane < 64, packed[:half], roll(packed[half:], 64))
    for i in range(out_ref.shape[0]):
        out_ref[i] = folded


def rotate_kernel(in_ref, stack_ref, out_ref):
    orbitals = out_ref.shape[0]
    folded = in_ref[0]
    for i in range(1, in_ref.shape[0]):
        folded = folded + in_ref[i]
    lane = lanes_of(orbitals)
    row = lax.broadcasted_iota(jnp.int32, (orbitals, LANES), 0)
    packed = jnp.concatenate([folded, roll(folded, 64)], axis=0)
    packed = jnp.where(lane < orbitals, packed, 0.0)
    square = jnp.concatenate(
        [packed, jnp.zeros((LANES - orbitals, LANES), jnp.float32)], axis=0
    )
    flipped = square.T[:orbitals]
    real = jnp.where(row <= lane, packed, flipped)
    imaginary = jnp.where(row < lane, -flipped, jnp.where(row > lane, packed, 0.0))
    diagonal = row == lane
    components = ROWS * 2 * NX
    trace = jnp.sum(jnp.where(diagonal, real, 0.0), keepdims=True)
    mean_square = trace / (orbitals * components) + 1e-06
    shrink = 0.5 / (components * mean_square)
    inverse = 1.0 / jnp.sqrt(mean_square)
    inside = lane < orbitals
    over_self = jnp.where(diagonal, 1.5, 0.0) - shrink * real
    over_turned = -shrink * imaginary
    left = jnp.where(inside, over_self, 0.0) + roll(jnp.where(inside, over_turned, 0.0), 64)
    high, low = split(left * inverse)
    left = jnp.concatenate(
        [
            jnp.concatenate([high, high], axis=1),
            jnp.concatenate([low, jnp.zeros_like(low)], axis=1),
        ],
        axis=0,
    )
    for q in range(5):
        right = jnp.concatenate([stack_ref[5 * q + t] for t in range(5)], axis=1)
        both = mul(left, right)
        out_ref[:, 640 * q : 640 * (q + 1)] = both[:orbitals] + both[orbitals:]


def shaped(shape, dtype=jnp.float32):
    return jax.ShapeDtypeStruct(shape, dtype)


def call(body, kinds, outs, scratch=(), limit=48):
    spaces = {"s": pltpu.SMEM, "v": pltpu.VMEM}
    many = isinstance(outs, (list, tuple))
    one = pl.BlockSpec(memory_space=pltpu.VMEM)
    return pl.pallas_call(
        body,
        out_shape=outs,
        in_specs=[pl.BlockSpec(memory_space=spaces[k]) for k in kinds],
        out_specs=(one,) * len(outs) if many else one,
        scratch_shapes=list(scratch),
        compiler_params=pltpu.CompilerParams(vmem_limit_bytes=limit << 20),
    )


def field_scratch():
    return pltpu.VMEM((ROWS, WIDE), jnp.float32)


def run_density(rank, weight, occupation, slots, vector, linear, table):
    field = shaped((ROWS, WIDE))
    return call(
        density_kernel,
        "sssssvvvvv",
        (field, field, field, shaped((GROUP * NZ, LANES))),
        (
            pltpu.VMEM((2, ROWS, LANES), jnp.float32),
            pltpu.VMEM((2, WIDE, WIDE), jnp.bfloat16),
            pltpu.VMEM((ROWS, LANES), jnp.float32),
        ),
    )(
        rank, weight, occupation, slots, vector, linear,
        table["x_second"], table["x_first"], table["x_magic"], table["y_all"],
    )


def run_total(values, count):
    return call(total_kernel, "v", shaped((count,) + values.shape[1:]))(values)


def run_potential(values, external, core):
    return call(
        potential_kernel,
        "vvv",
        (shaped(external.shape), shaped((GROUP, NZ, LANES))),
        (pltpu.VMEM((NZ, LANES), jnp.float32),),
    )(values, external, core)


def run_filter(counts, vector, field, kinetic, smooth, slabs, table):
    return call(
        filter_kernel,
        "ssvvvvvvvvvv",
        shaped((GROUP * 25, LANES)),
        (
            pltpu.VMEM((ROWS, LANES), jnp.float32),
            pltpu.VMEM((2, WIDE, WIDE), jnp.bfloat16),
            field_scratch(),
            field_scratch(),
            field_scratch(),
            field_scratch(),
            pltpu.VMEM((2, ROWS + 24, LANES), jnp.float32),
            pltpu.VMEM((2, GROUP * 24, LANES), jnp.float32),
        ),
    )(
        counts, vector, field, kinetic, smooth, slabs,
        table["x_second"], table["x_first"], table["x_magic"], table["x_magic_back"],
        table["y_all"], table["y_back"],
    )


def run_gram(rank, counts, slots, received):
    orbitals = slots.shape[0]
    return call(
        gram_kernel,
        "sssv",
        (shaped((25, WIDE, LANES), jnp.bfloat16), shaped((8, orbitals // 2, LANES))),
        (pltpu.VMEM((25 * orbitals, LANES), jnp.float32),),
    )(rank, counts, slots, received)


def run_rotate(values, stack, orbitals):
    return call(rotate_kernel, "vv", shaped((orbitals, 25 * LANES)))(values, stack)


def exchange(values, axes):
    return lax.all_to_all(values, axes, split_axis=0, concat_axis=0, tiled=True)


def on_device(
    wavefunctions,
    kpoint_vector,
    kpoint_weight,
    occupation,
    orbital_slot,
    piece_rows,
    external_potential,
    core_density,
):
    kpt, orb = ("kpt",), ("orb_y", "orb_z")
    rank = lax.axis_index(orb).astype(jnp.int32).reshape(1)
    table = {name: jnp.asarray(value) for name, value in tables().items()}
    field, kinetic, smooth, partial_density = run_density(
        rank, kpoint_weight, occupation, orbital_slot, kpoint_vector,
        wavefunctions.reshape(-1, LANES), table,
    )
    terms = exchange(partial_density.reshape(GROUP, NZ, LANES), orb)
    terms = exchange(run_total(terms, 8), kpt)
    density, slabs = run_potential(terms, external_potential, core_density)
    slabs = exchange(slabs, orb).reshape(GROUP * NZ, LANES)
    outgoing = run_filter(piece_rows, kpoint_vector, field, kinetic, smooth, slabs, table)
    received = exchange(outgoing.reshape(GROUP, 25 * LANES), orb).reshape(GROUP * 25, LANES)
    stack, packed = run_gram(rank, piece_rows, orbital_slot, received)
    packed = exchange(packed, ("orb_z",))
    packed = exchange(run_total(packed, 8), ("orb_y",))
    return (density, run_rotate(packed, stack, orbital_slot.shape[0])[None])


def solution(mesh):
    side = math.isqrt(mesh.shape["orb"])
    fine = Mesh(
        mesh.devices.reshape(mesh.shape["kpt"], -1, side), ("kpt", "orb_y", "orb_z")
    )
    orb = ("orb_y", "orb_z")
    in_specs = (
        P("kpt", orb, None),
        P("kpt", None),
        P("kpt"),
        P(),
        P(),
        P(),
        P(None, orb),
        P(None, orb),
    )
    out_specs = (P(None, orb), P("kpt", None, orb))
    return jax.shard_map(
        on_device, mesh=fine, in_specs=in_specs, out_specs=out_specs, check_vma=False
    )
```

```python
import functools
import math

import jax
import jax.numpy as jnp
import numpy as np
from jax import lax
from jax.experimental import pallas as pl
from jax.experimental.pallas import tpu as pltpu
from jax.sharding import Mesh
from jax.sharding import PartitionSpec as P

NX = 80
NY = 80
NZ = 8
ROWS = NZ * NY
LANES = 128
WIDE = 2 * LANES
SLAB = 100
GROUP = 64

magic_taps = (
    8.433424733352934e-07,
    -1.290557201342061e-05,
    8.76298447621056e-05,
    -0.00030158038132690465,
    0.001747237136729939,
    -0.009420470302010804,
    0.023738214637249424,
    0.0612625895831208,
    0.9940415697834004,
    -0.06048952891969835,
    -0.021030251609303816,
    0.013372634148547948,
    -0.0034412814449349387,
    0.0004944322768868992,
    -5.185986881173433e-05,
    2.7273449291197967e-06,
)
grid_step = 0.9
half_order = 14
spectrum_center = 13.0
spectrum_half = 17.0
exchange_coef = (3.0 / math.pi) ** (1.0 / 3.0)


def stencil_taps():
    factorial = math.factorial
    second_taps = {}
    first_taps = {}
    running = 0.0
    for offset in range(1, half_order + 1):
        weight_j = factorial(half_order) ** 2 / (
            factorial(half_order - offset) * factorial(half_order + offset)
        )
        tap_sign = (-1.0) ** (offset + 1)
        second_taps[offset] = 2.0 * tap_sign * weight_j / offset**2
        second_taps[-offset] = second_taps[offset]
        first_taps[offset] = tap_sign * weight_j / offset
        first_taps[-offset] = -first_taps[offset]
        running = running + 2.0 * second_taps[offset]
    second_taps[0] = -running
    return (second_taps, first_taps)


def band_matrix(length, taps):
    matrix = np.zeros((length, length))
    for offset, tap_value in taps.items():
        matrix = matrix + tap_value * np.eye(length, k=offset)
    return matrix


def axis_tables(length):
    second_taps, first_taps = stencil_taps()
    magic_band = band_matrix(
        length, {tap_index - 8: magic_taps[tap_index] for tap_index in range(16)}
    )
    return (
        band_matrix(length, second_taps) * (-0.5 / grid_step**2),
        band_matrix(length, first_taps) / grid_step,
        magic_band,
    )


def split_table(matrix):
    matrix = np.asarray(matrix, np.float32)
    high = matrix.astype(jnp.bfloat16)
    low = (matrix - high.astype(np.float32)).astype(jnp.bfloat16)
    return high, low


def padded(block):
    table = np.zeros((LANES, LANES))
    table[:NX, :NX] = block
    return table


def tables():
    second_x, first_x, magic_x = axis_tables(NX)
    second_y, first_y, magic_y = axis_tables(NY)

    def packed(matrix):
        high, low = split_table(matrix)
        return np.concatenate([high, low, high], axis=1)

    return {
        "x_kinetic": np.stack([padded(second_x.T), padded(first_x.T)]).astype(np.float32),
        "x_magic": np.stack(split_table(padded(magic_x.T))),
        "x_back": np.stack(split_table(padded(magic_x))),
        "y_all": packed(np.concatenate([magic_y, second_y, first_y], axis=0)),
        "y_back": packed(magic_y.T),
    }


def split(values):
    high = values.astype(jnp.bfloat16)
    low = (values - high.astype(jnp.float32)).astype(jnp.bfloat16)
    return high, low


def mul(left, right):
    return jnp.dot(left, right, preferred_element_type=jnp.float32)


def twist(values):
    return jnp.concatenate([values[:, LANES:], -values[:, :LANES]], axis=1)


def lanes_of(rows):
    return lax.broadcasted_iota(jnp.int32, (rows, LANES), 1)


def roll(values, shift):
    shift = shift % LANES
    return pltpu.roll(values, shift, 1) if shift else values


def compose(lane, parts):
    result = parts[-1][1]
    for end, values in reversed(parts[:-1]):
        result = jnp.where(lane < end, values, result)
    return result


def both_halves(table):
    zero = jnp.zeros_like(table)
    return jnp.concatenate(
        [jnp.concatenate([table, zero], axis=1), jnp.concatenate([zero, table], axis=1)], axis=0
    )


def x_weights(vector_ref, table_ref, weight_ref):
    qx, qy, qz = (vector_ref[0, d] for d in range(3))
    shift = 0.5 * (qx * qx + qy * qy + qz * qz)
    row = lax.broadcasted_iota(jnp.int32, (LANES, LANES), 0)
    column = lax.broadcasted_iota(jnp.int32, (LANES, LANES), 1)
    same_high, same_low = split(table_ref[0] + jnp.where(row == column, shift, 0.0))
    cross_high, cross_low = split(qx * table_ref[1])
    for i, (same, cross) in enumerate([(same_high, cross_high), (same_low, cross_low)]):
        weight_ref[i, :LANES, :LANES] = same
        weight_ref[i, LANES:, LANES:] = same
        weight_ref[i, LANES:, :LANES] = cross
        weight_ref[i, :LANES, LANES:] = -cross


def x_product(values, weight_ref):
    high, low = split(values)
    return mul(high, weight_ref[0]) + mul(high, weight_ref[1]) + mul(low, weight_ref[0])


def y_product(table_ref, values):
    high, low = split(values)
    return mul(table_ref[...], jnp.concatenate([high, high, low], axis=0))


CHUNK = 160


def forward_xy(vector_ref, field_ref, kinetic_ref, smooth_ref, y_all_ref, weight_ref, x_magic_ref):
    qy = vector_ref[0, 1]
    for z in range(NZ):
        rows = slice(z * NY, (z + 1) * NY)
        product = y_product(y_all_ref, field_ref[rows, :])
        smooth_ref[rows, :] = product[:NY]
        kinetic_ref[rows, :] = product[NY : 2 * NY] + twist(qy * product[2 * NY :])
    for start in range(0, ROWS, CHUNK):
        rows = slice(start, start + CHUNK)
        kinetic_ref[rows, :] += x_product(field_ref[rows, :], weight_ref)
        smooth_ref[rows, :] = x_product(smooth_ref[rows, :], x_magic_ref)


def z_sum(matrix, planes):
    results = []
    for v in range(NZ):
        total = None
        for z in range(NZ):
            if matrix[v, z] != 0.0:
                term = float(matrix[v, z]) * planes[z]
                total = term if total is None else total + term
        results.append(total)
    return results


def z_kinetic(vector_ref, field_ref, kinetic_ref, y):
    second_z, first_z, _ = axis_tables(NZ)
    qz = vector_ref[0, 2]
    planes = [field_ref[z * NY + y : z * NY + y + 8, :] for z in range(NZ)]
    turned = [qz * twist(p) for p in planes]
    for z, (a, b) in enumerate(zip(z_sum(second_z, planes), z_sum(first_z, turned))):
        kinetic_ref[z * NY + y : z * NY + y + 8, :] += a + b


def density_kernel(
    axes,
    weight_k_hbm,
    occupation_hbm,
    slot_hbm,
    vector_hbm,
    linear_hbm,
    x_kinetic_hbm,
    x_magic_hbm,
    y_all_hbm,
    field_ref,
    kinetic_ref,
    smooth_ref,
    weight_ref,
    out_ref,
    weight_k_ref,
    occupation_ref,
    slot_ref,
    vector_ref,
    linear_ref,
    x_kinetic_ref,
    x_half_ref,
    y_all_ref,
    parts_ref,
    x_magic_ref,
    rows_ref,
    arrived,
):
    copies = [
        pltpu.make_async_copy(source, target, arrived.at[i])
        for i, (source, target) in enumerate(
            [
                (linear_hbm, linear_ref),
                (vector_hbm, vector_ref),
                (x_kinetic_hbm, x_kinetic_ref),
                (x_magic_hbm, x_half_ref),
                (y_all_hbm, y_all_ref),
                (weight_k_hbm, weight_k_ref),
                (occupation_hbm, occupation_ref),
                (slot_hbm, slot_ref),
            ]
        )
    ]
    for copy in copies:
        copy.start()
    for copy in copies:
        copy.wait()
    rank = lax.axis_index(axes) if axes else 0
    x_weights(vector_ref, x_kinetic_ref, weight_ref)
    for i in range(2):
        x_magic_ref[i] = both_halves(x_half_ref[i])
    lane = lanes_of(ROWS // 4)
    tiles = [linear_ref[pl.ds(t, ROWS // 4, stride=5), :] for t in range(5)]
    for h in range(8):
        t, start = divmod(NX * h, LANES)
        base = tiles[t]
        if start + NX > LANES:
            base = jnp.where(lane >= start, base, tiles[t + 1])
        piece = jnp.where(lane < NX, roll(base, -start), 0.0)
        parts_ref[h % 2, pl.ds(h // 2, ROWS // 4, stride=4), :] = piece
    field_ref[:, :LANES] = parts_ref[0]
    field_ref[:, LANES:] = parts_ref[1]
    forward_xy(
        vector_ref, field_ref, kinetic_ref, smooth_ref, y_all_ref, weight_ref, x_magic_ref
    )
    scale = jnp.float32(0.0)
    for i in range(slot_ref.shape[0]):
        scale = scale + jnp.where(slot_ref[i] == rank, occupation_ref[i], 0.0)
    scale = scale * weight_k_ref[0]
    magic_z = axis_tables(NZ)[2]
    for y in range(0, NY, 8):
        z_kinetic(vector_ref, field_ref, kinetic_ref, y)
        planes = [smooth_ref[z * NY + y : z * NY + y + 8, :] for z in range(NZ)]
        for z, plane in enumerate(z_sum(magic_z, planes)):
            smooth_ref[z * NY + y : z * NY + y + 8, :] = plane
            real, imaginary = plane[:, :LANES], plane[:, LANES:]
            rows_ref[z * NY + y : z * NY + y + 8, :] = scale * (
                real * real + imaginary * imaginary
            )
    groups = ROWS // 5
    lane = lanes_of(groups)
    rows = [rows_ref[pl.ds(t, groups, stride=5), :] for t in range(5)]
    for s in range(4):
        slab = jnp.where(
            lane < NX * (s + 1) - SLAB * s,
            roll(rows[s], NX * s - SLAB * s),
            roll(rows[s + 1], NX * (s + 1) - SLAB * s),
        )
        last = slab[16 * (NZ - 1) :]
        for z in range(NZ - 1):
            tile = slab[16 * z : 16 * z + 16]
            if z < 4:
                tile = jnp.where(lane[:16] < SLAB, tile, roll(last, SLAB - 25 * z))
            out_ref[pl.ds(7 * s + z, 16, stride=28), :] = tile


def first_total_kernel(in_ref, out_ref):
    total = in_ref[:56, :]
    for i in range(1, GROUP // 8):
        total = total + in_ref[56 * i : 56 * (i + 1), :]
    rows = total[:7]
    for i in range(1, 8):
        rows = rows + total[7 * i : 7 * (i + 1)]
    for i in range(out_ref.shape[0]):
        out_ref[i, :7, :] = rows
        out_ref[i, 7:, :] = jnp.zeros((1, LANES), jnp.float32)


def total_kernel(in_ref, out_ref):
    total = in_ref[0]
    for i in range(1, in_ref.shape[0]):
        total = total + in_ref[i]
    for i in range(out_ref.shape[0]):
        out_ref[i] = total


def last_plane(lane, rows):
    return compose(lane, [(25 * (c + 1), roll(rows[c], 25 * c - SLAB)) for c in range(4)])


def potential_kernel(in_ref, external_ref, core_ref, density_ref, out_ref, pad_ref, many_ref):
    total = in_ref[0]
    for i in range(1, in_ref.shape[0]):
        total = total + in_ref[i]
    pad_ref[...] = total
    one = lanes_of(1)
    pad_ref[7:, :] = last_plane(one, [total[c : c + 1] for c in range(4)])
    density = pad_ref[:, :SLAB]
    density_ref[...] = density
    root = jnp.exp(jnp.log(density + core_ref[...]) * (1.0 / 3.0))
    pad_ref[:, SLAB:] = jnp.zeros((NZ, LANES - SLAB), jnp.float32)
    pad_ref[:, :SLAB] = external_ref[...] - exchange_coef * root
    last = pad_ref[7:, :]
    for c in range(4):
        row = pad_ref[c : c + 1, :]
        pad_ref[c : c + 1, :] = jnp.where(one < SLAB, row, roll(last, SLAB - 25 * c))
    rows = pad_ref[:7, :]
    for i in range(8):
        many_ref[7 * i : 7 * (i + 1), :] = rows
    many = many_ref[...]
    for i in range(GROUP // 8):
        out_ref[56 * i : 56 * (i + 1), :] = many


def filter_kernel(
    count_ref,
    vector_ref,
    field_ref,
    kinetic_ref,
    smooth_ref,
    weight_ref,
    slabs_ref,
    x_half_ref,
    x_half_back_ref,
    y_all_ref,
    y_back_ref,
    out_ref,
    potential_ref,
    x_magic_ref,
    x_back_ref,
    term_ref,
    wave_ref,
    kin_ref,
    work_ref,
    parts_ref,
    owned_ref,
):
    for i in range(2):
        x_magic_ref[i] = both_halves(x_half_ref[i])
        x_back_ref[i] = both_halves(x_half_back_ref[i])
    lane = lanes_of(16)
    planes = [
        [slabs_ref[pl.ds(7 * s + z, 16, stride=28), :] for s in range(4)] for z in range(NZ - 1)
    ]
    planes.append([last_plane(lane, [planes[c][s] for c in range(4)]) for s in range(4)])
    for z, slabs in enumerate(planes):
        for t in range(5):
            if t == 0:
                row = slabs[0]
            elif t == 4:
                row = roll(slabs[3], SLAB * 3 - NX * 4)
            else:
                row = jnp.where(
                    lane < SLAB * t - NX * t,
                    roll(slabs[t - 1], SLAB * (t - 1) - NX * t),
                    roll(slabs[t], SLAB * t - NX * t),
                )
            potential_ref[pl.ds(z * NY + t, 16, stride=5), :] = row
    magic_z = axis_tables(NZ)[2]

    def weighted(planes, y):
        result = []
        for z, plane in enumerate(planes):
            potential = potential_ref[z * NY + y : z * NY + y + 8, :]
            result.append(plane * jnp.concatenate([potential, potential], axis=1))
        return result

    def backward(values_ref):
        for z in range(NZ):
            rows = slice(z * NY, (z + 1) * NY)
            values_ref[rows, :] = y_product(y_back_ref, values_ref[rows, :])

    for y in range(0, NY, 8):
        planes = [smooth_ref[z * NY + y : z * NY + y + 8, :] for z in range(NZ)]
        for z, plane in enumerate(z_sum(magic_z.T, weighted(planes, y))):
            work_ref[z * NY + y : z * NY + y + 8, :] = plane
    backward(work_ref)
    for start in range(0, ROWS, CHUNK):
        rows = slice(start, start + CHUNK)
        applied = kinetic_ref[rows, :] + x_product(work_ref[rows, :], x_back_ref)
        term_ref[rows, :] = (applied - spectrum_center * field_ref[rows, :]) * (
            1.0 / spectrum_half
        )
    forward_xy(vector_ref, term_ref, kin_ref, wave_ref, y_all_ref, weight_ref, x_magic_ref)
    for y in range(0, NY, 8):
        z_kinetic(vector_ref, term_ref, kin_ref, y)
        planes = [wave_ref[z * NY + y : z * NY + y + 8, :] for z in range(NZ)]
        planes = weighted(z_sum(magic_z, planes), y)
        for z, plane in enumerate(z_sum(magic_z.T, planes)):
            work_ref[z * NY + y : z * NY + y + 8, :] = plane
    backward(work_ref)
    for start in range(0, ROWS, CHUNK):
        rows = slice(start, start + CHUNK)
        image = kin_ref[rows, :] + x_product(work_ref[rows, :], x_back_ref)
        image = image - spectrum_center * term_ref[rows, :]
        filtered = (2.0 / spectrum_half) * image - field_ref[rows, :]
        parts_ref[0, rows, :] = filtered[:, :LANES]
        parts_ref[1, rows, :] = filtered[:, LANES:]
    parts_ref[:, ROWS:, :] = jnp.zeros((2, parts_ref.shape[1] - ROWS, LANES), jnp.float32)
    offset = 0
    for d in range(GROUP):
        for part in range(2):
            owned_ref[part, 24 * d : 24 * d + 24, :] = parts_ref[part, pl.ds(offset, 24), :]
        offset = offset + count_ref[d]
    lane = lanes_of(GROUP)
    for q in range(5):
        pieces = [
            roll(owned_ref[h % 2, pl.ds(4 * q + h // 2, GROUP, stride=24), :], NX * h)
            for h in range(8)
        ]
        for t in range(5):
            first, last = LANES * t // NX, (LANES * t + LANES - 1) // NX
            parts = [(NX * (h + 1) - LANES * t, pieces[h]) for h in range(first, last + 1)]
            out_ref[pl.ds(5 * q + t, GROUP, stride=25), :] = compose(lane, parts)


def gram_kernel(axes, count_ref, slot_ref, in_ref, stack_ref, out_ref, chosen_ref):
    orbitals = slot_ref.shape[0]
    for i in range(orbitals):
        chosen_ref[pl.ds(i, 25, stride=orbitals), :] = in_ref[pl.ds(25 * slot_ref[i], 25), :]
    limit = 2 * NX * count_ref[lax.axis_index(axes) if axes else 0]
    lane = lanes_of(orbitals)
    total = jnp.zeros((2 * orbitals, WIDE), jnp.float32)
    empty = jnp.zeros((64 - orbitals, LANES), jnp.bfloat16)
    for q in range(5):
        tiles = []
        for t in range(5):
            place = 5 * q + t
            tile = chosen_ref[place * orbitals : (place + 1) * orbitals, :]
            tiles.append(jnp.where(lane < limit - LANES * place, tile, 0.0))
        ahead = [roll(tile, -NX) for tile in tiles]
        behind = [roll(tile, NX) for tile in tiles]
        lefts, rights = [], []
        for t in range(5):
            parts, position = [], LANES * t
            while position < LANES * (t + 1):
                h = position // NX
                shift = NX if h % 2 == 0 else -NX
                source = (position + shift) // LANES
                end = min(
                    NX * (h + 1), LANES * (source + 1) - shift, LANES * (t + 1)
                )
                values = ahead[source] if h % 2 == 0 else -behind[source]
                parts.append((end - LANES * t, values))
                position = end
            turned = compose(lane, parts)
            high, low = split(tiles[t])
            turned_high, turned_low = split(turned)
            right = jnp.concatenate(
                [high, empty, turned_high, empty, low, empty, turned_low, empty], axis=0
            )
            stack_ref[5 * q + t] = right
            lefts.append(jnp.concatenate([high, low], axis=0))
            rights.append(right)
        total = total + lax.dot_general(
            jnp.concatenate(lefts, axis=1),
            jnp.concatenate(rights, axis=1),
            (((1,), (1,)), ((), ())),
            preferred_element_type=jnp.float32,
        )
    both = total[:orbitals, :LANES] + (
        total[orbitals:, :LANES] + total[:orbitals, LANES:]
    )
    row = lax.broadcasted_iota(jnp.int32, (orbitals, LANES), 0)
    packed = jnp.where(row <= lane, both, roll(both, 64))
    half = orbitals // 2
    lane = lanes_of(half)
    folded = jnp.where(lane < 64, packed[:half], roll(packed[half:], 64))
    for i in range(out_ref.shape[0]):
        out_ref[i] = folded


def rotate_kernel(in_ref, stack_ref, out_ref):
    orbitals = out_ref.shape[0]
    folded = in_ref[0]
    for i in range(1, in_ref.shape[0]):
        folded = folded + in_ref[i]
    lane = lanes_of(orbitals)
    row = lax.broadcasted_iota(jnp.int32, (orbitals, LANES), 0)
    packed = jnp.concatenate([folded, roll(folded, 64)], axis=0)
    packed = jnp.where(lane < orbitals, packed, 0.0)
    square = jnp.concatenate(
        [packed, jnp.zeros((LANES - orbitals, LANES), jnp.float32)], axis=0
    )
    flipped = square.T[:orbitals]
    real = jnp.where(row <= lane, packed, flipped)
    imaginary = jnp.where(row < lane, -flipped, jnp.where(row > lane, packed, 0.0))
    diagonal = row == lane
    components = ROWS * 2 * NX
    trace = jnp.sum(jnp.where(diagonal, real, 0.0), keepdims=True)
    mean_square = trace / (orbitals * components) + 1e-06
    shrink = 0.5 / (components * mean_square)
    inverse = 1.0 / jnp.sqrt(mean_square)
    inside = lane < orbitals
    over_self = jnp.where(diagonal, 1.5, 0.0) - shrink * real
    over_turned = -shrink * imaginary
    left = jnp.where(inside, over_self, 0.0) + roll(jnp.where(inside, over_turned, 0.0), 64)
    high, low = split(left * inverse)
    left = jnp.concatenate(
        [
            jnp.concatenate([high, high], axis=1),
            jnp.concatenate([low, jnp.zeros_like(low)], axis=1),
        ],
        axis=0,
    )
    for q in range(5):
        right = jnp.concatenate([stack_ref[5 * q + t] for t in range(5)], axis=1)
        both = mul(left, right)
        out_ref[:, 640 * q : 640 * (q + 1)] = both[:orbitals] + both[orbitals:]


def shaped(shape, dtype=jnp.float32):
    return jax.ShapeDtypeStruct(shape, dtype)


def call(body, kinds, outs, scratch=(), limit=48):
    spaces = {"s": pltpu.SMEM, "v": pltpu.VMEM, "h": pltpu.HBM}
    many = isinstance(outs, (list, tuple))
    one = pl.BlockSpec(memory_space=pltpu.VMEM)
    return pl.pallas_call(
        body,
        out_shape=outs,
        in_specs=[pl.BlockSpec(memory_space=spaces[k]) for k in kinds],
        out_specs=(one,) * len(outs) if many else one,
        scratch_shapes=list(scratch),
        compiler_params=pltpu.CompilerParams(vmem_limit_bytes=limit << 20),
    )


def vmem(*shape, dtype=jnp.float32):
    return pltpu.VMEM(shape, dtype)


def run_density(axes, weight, occupation, slots, vector, linear, table):
    field = shaped((ROWS, WIDE))
    tables = [table[name] for name in ("x_kinetic", "x_magic", "y_all")]
    return call(
        functools.partial(density_kernel, axes),
        "hhhhhhhh",
        (field, field, field, shaped((2, WIDE, WIDE), jnp.bfloat16), shaped((GROUP * 7, LANES))),
        (
            pltpu.SMEM(weight.shape, weight.dtype),
            pltpu.SMEM(occupation.shape, occupation.dtype),
            pltpu.SMEM(slots.shape, slots.dtype),
            pltpu.SMEM(vector.shape, vector.dtype),
            vmem(*linear.shape),
            *(vmem(*t.shape, dtype=t.dtype) for t in tables),
            vmem(2, ROWS, LANES),
            vmem(2, WIDE, WIDE, dtype=jnp.bfloat16),
            vmem(ROWS, LANES),
            pltpu.SemaphoreType.DMA((8,)),
        ),
    )(weight, occupation, slots, vector, linear, *tables)


def run_first_total(values, count):
    return call(first_total_kernel, "v", shaped((count, NZ, LANES)))(values)


def run_total(values, count):
    return call(total_kernel, "v", shaped((count,) + values.shape[1:]))(values)


def run_potential(values, external, core):
    return call(
        potential_kernel,
        "vvv",
        (shaped(external.shape), shaped((GROUP * 7, LANES))),
        (vmem(NZ, LANES), vmem(56, LANES)),
    )(values, external, core)


def run_filter(counts, vector, field, kinetic, smooth, weights, slabs, table):
    tables = [table[name] for name in ("x_magic", "x_back", "y_all", "y_back")]
    return call(
        filter_kernel,
        "ssvvvvvvvvv",
        shaped((GROUP * 25, LANES)),
        (
            vmem(ROWS, LANES),
            vmem(2, WIDE, WIDE, dtype=jnp.bfloat16),
            vmem(2, WIDE, WIDE, dtype=jnp.bfloat16),
            *(vmem(ROWS, WIDE) for _ in range(4)),
            vmem(2, ROWS + 24, LANES),
            vmem(2, GROUP * 24, LANES),
        ),
    )(counts, vector, field, kinetic, smooth, weights, slabs, *tables)


def run_gram(axes, counts, slots, received):
    orbitals = slots.shape[0]
    return call(
        functools.partial(gram_kernel, axes),
        "ssv",
        (shaped((25, WIDE, LANES), jnp.bfloat16), shaped((8, orbitals // 2, LANES))),
        (vmem(25 * orbitals, LANES),),
    )(counts, slots, received)


def run_rotate(values, stack, orbitals):
    return call(rotate_kernel, "vv", shaped((orbitals, 25 * LANES)))(values, stack)


def exchange(values, axes):
    return lax.all_to_all(values, axes, split_axis=0, concat_axis=0, tiled=True)


def on_device(
    wavefunctions,
    kpoint_vector,
    kpoint_weight,
    occupation,
    orbital_slot,
    piece_rows,
    external_potential,
    core_density,
):
    kpt, orb = ("kpt",), ("orb_y", "orb_z")
    table = {name: jnp.asarray(value) for name, value in tables().items()}
    field, kinetic, smooth, weights, partial_density = run_density(
        orb, kpoint_weight, occupation, orbital_slot, kpoint_vector,
        wavefunctions.reshape(-1, LANES), table,
    )
    terms = exchange(partial_density.reshape(GROUP, 7 * LANES), orb)
    terms = exchange(run_first_total(terms.reshape(GROUP * 7, LANES), 8), kpt)
    density, slabs = run_potential(terms, external_potential, core_density)
    slabs = exchange(slabs.reshape(GROUP, 7 * LANES), orb).reshape(GROUP * 7, LANES)
    outgoing = run_filter(
        piece_rows, kpoint_vector, field, kinetic, smooth, weights, slabs, table
    )
    received = exchange(outgoing.reshape(GROUP, 25 * LANES), orb).reshape(GROUP * 25, LANES)
    stack, packed = run_gram(orb, piece_rows, orbital_slot, received)
    packed = exchange(packed, ("orb_z",))
    packed = exchange(run_total(packed, 8), ("orb_y",))
    return (density, run_rotate(packed, stack, orbital_slot.shape[0])[None])


def solution(mesh):
    side = math.isqrt(mesh.shape["orb"])
    fine = Mesh(
        mesh.devices.reshape(mesh.shape["kpt"], -1, side), ("kpt", "orb_y", "orb_z")
    )
    orb = ("orb_y", "orb_z")
    in_specs = (
        P("kpt", orb, None),
        P("kpt", None),
        P("kpt"),
        P(),
        P(),
        P(),
        P(None, orb),
        P(None, orb),
    )
    out_specs = (P(None, orb), P("kpt", None, orb))
    return jax.shard_map(
        on_device, mesh=fine, in_specs=in_specs, out_specs=out_specs, check_vma=False
    )
```
